256 devices in a mesh: row: 16 (over x, z_lo, core), col: 4 (over y), rep: 4 (over z_hi).
Axes of the slice: x: 4, y: 4, z: 8 (z_hi: 4, z_lo: 2; z = z_hi * 2 + z_lo), core: 2. Of those that a mesh axis runs over, the one named last changes fastest.
Arguments:
- a_values: float32 [16, 4, 4, 192, 128, 128], P('row', 'col', 'rep'), may hold values from -6 to 6
- b_values: float32 [16, 4, 4, 16, 128, 128], P('row', 'col', 'rep'), may hold values from -0.125 to 0.125
- a_live: int32 [16, 4, 4, 192], P('row', 'col', 'rep'), may hold values from 0 to 1, as said below
- b_live: int32 [16, 4, 4, 16], P('row', 'col', 'rep'), may hold values from 0 to 1, as said below
- triples: int32 [16, 4, 4, 2, 3, 256], P('row', 'col', 'rep'), may hold values from 0 to 191, as said below
Outputs:
- product_blocks: float32 [16, 4, 48, 128, 128], P('row', 'col', 'rep')
The draws below stay inside these ranges and needn't reach their ends.
Inputs may be any that keep to these rules, and one draw needn't show every extreme that they name: `a_live`: each tile has at most 96 occupied slots and at least half as many; some tile has exactly 96. `b_live`: each tile has at most 8 occupied slots and at least half as many; some tile has exactly 8. `triples`: in each table the live entries come first, at least 64 of them; some table is full; left slots are below 192, right slots below 16, product slots at most 48; padding entries have product slot 48 and left and right slots 0.
All inputs are finite; a program needn't handle non-finite values.
Results may differ from the reference program's by a relative error of at most 0.0003.
Values sent between devices are 32-bit elements; how exact they have to be, the bound alone decides.
No kernel may reach another device: no remote copies, remote signals or barrier semaphores. Data moves between devices by JAX's collectives and lax.ppermute only.
A program may use at most 128 MiB of HBM per device.

```python
import jax
import jax.numpy as jnp
from jax import lax

BS = 128
A_SLOTS = 192
B_SLOTS = 16
C_SLOTS = 48
BATCH = 256
N_ROW = 16
N_COL = 4
N_REP = 4


def live_mask(key, slots, most):
    tiles = N_ROW * N_COL * N_REP
    subkeys = jax.random.split(key, 3)
    counts = jax.random.randint(subkeys[0], (tiles,), most // 2, most + 1)
    fullest = jax.random.randint(subkeys[1], (), 0, tiles)
    counts = jnp.where(jnp.arange(tiles) == fullest, most, counts)
    scores = jax.random.randint(subkeys[2], (tiles, slots), 0, 2 ** 20) * slots + jnp.arange(slots)[None, :]
    ranks = jnp.argsort(jnp.argsort(scores, axis=1), axis=1)
    return (ranks < counts[:, None]).astype(jnp.int32).reshape(N_ROW, N_COL, N_REP, slots)


def draw_a_live(key, part):
    key = jax.random.fold_in(key, 3)
    return live_mask(key, A_SLOTS, A_SLOTS // 2)


def draw_b_live(key, part):
    key = jax.random.fold_in(key, 5)
    return live_mask(key, B_SLOTS, B_SLOTS // 2)


def draw_triples(key, part):
    key = jax.random.fold_in(key, 11)
    tables = N_ROW * N_COL * N_REP * 2
    subkeys = jax.random.split(key, 5)
    counts = jax.random.randint(subkeys[0], (tables,), BATCH // 4, BATCH + 1)
    fullest = jax.random.randint(subkeys[1], (), 0, tables)
    counts = jnp.where(jnp.arange(tables) == fullest, BATCH, counts)
    left_slots = jax.random.randint(subkeys[2], (tables, BATCH), 0, A_SLOTS)
    right_slots = jax.random.randint(subkeys[3], (tables, BATCH), 0, B_SLOTS)
    product_slots = jax.random.randint(subkeys[4], (tables, BATCH), 0, C_SLOTS)
    filled = jnp.arange(BATCH)[None, :] < counts[:, None]
    left_slots = jnp.where(filled, left_slots, 0)
    right_slots = jnp.where(filled, right_slots, 0)
    product_slots = jnp.where(filled, product_slots, C_SLOTS)
    stacked = jnp.stack([left_slots, right_slots, product_slots], axis=1).astype(jnp.int32)
    return stacked.reshape(N_ROW, N_COL, N_REP, 2, 3, BATCH)


def shard_levels(own_key, extent, cuts, least, high):
    def one(dim, parts):
        heights = jax.random.uniform(jax.random.fold_in(jax.random.fold_in(own_key, 6), dim), (parts,), jnp.float32, least / len(cuts), high / len(cuts))
        return jnp.repeat(jnp.exp(heights), extent[dim] // parts).reshape((-1,) + (1,) * (len(extent) - dim - 1))

    factor_of = one(*cuts[0])
    for cut in cuts[1:]:
        factor_of = factor_of * one(*cut)
    return factor_of


def noise(own_key, dims, width, most, cuts=(), kind=jnp.bfloat16):
    result = width * jax.random.normal(own_key, dims, jnp.float32)
    if cuts:
        result = result * shard_levels(own_key, dims, cuts, -0.22, 0.18)
    return jnp.clip(result, -most, most).astype(kind)


def setup_inputs(seed: int = 0) -> dict:
    key_list = jax.random.split(jax.random.key(seed), 6)
    a_values = noise(key_list[0], (N_ROW, N_COL, N_REP, A_SLOTS, BS, BS), 1.0, 6.0, ((0, 16), (1, 4), (2, 4)), jnp.float32)
    b_values = noise(key_list[1], (N_ROW, N_COL, N_REP, B_SLOTS, BS, BS), (BS * 16) ** -0.5, 0.125, ((0, 16), (1, 4), (2, 4)), jnp.float32)
    a_live = draw_a_live(jax.random.fold_in(key_list[5], 71), 0)
    b_live = draw_b_live(jax.random.fold_in(key_list[5], 71), 0)
    triples = draw_triples(jax.random.fold_in(key_list[5], 71), 0)
    return dict(a_values=a_values, b_values=b_values, a_live=a_live, b_live=b_live, triples=triples)


def tile_products(left_tile, right_tile, table):
    totals = jnp.zeros((C_SLOTS + 1, BS, BS), jnp.float32)

    def advance(carry, entry):
        block_product = jnp.dot(left_tile[entry[0]], right_tile[entry[1]], precision=lax.Precision.HIGHEST, preferred_element_type=jnp.float32)
        return carry.at[entry[2]].add(block_product), None

    totals, _ = lax.scan(advance, totals, jnp.transpose(table).astype(jnp.int32))
    return totals[:C_SLOTS]


def reference(a_values, b_values, a_live, b_live, triples):
    left = a_values * a_live[..., None, None].astype(jnp.float32)
    right = b_values * b_live[..., None, None].astype(jnp.float32)

    def one_tile(flat_index):
        row_index = flat_index // N_COL
        col_index = flat_index % N_COL
        row_next = (row_index + 1) % N_ROW
        col_next = (col_index + 1) % N_COL

        def layer(layer_index):
            first = tile_products(left[row_index, col_index, layer_index], right[row_index, col_index, layer_index], triples[row_index, col_index, layer_index, 0])
            second = tile_products(left[row_next, col_index, layer_index], right[row_index, col_next, layer_index], triples[row_index, col_index, layer_index, 1])
            return first + second

        return jnp.sum(lax.map(layer, jnp.arange(N_REP, dtype=jnp.int32)), axis=0)

    tiles = lax.map(one_tile, jnp.arange(N_ROW * N_COL, dtype=jnp.int32))
    return tiles.reshape(N_ROW, N_COL, C_SLOTS, BS, BS)
```

```python
import jax
import jax.numpy as jnp
from jax import lax
from jax.experimental import pallas as pl
from jax.experimental.pallas import tpu as pltpu
from jax.sharding import PartitionSpec as P

BS = 128
C_SLOTS = 48
B_KEEP = 8
BATCH = 256
UNROLL = 8
f32 = jnp.float32
bf16 = jnp.bfloat16


def pack_kernel(live_ref, b_ref, out_ref, which, sems):
    for k in range(B_KEEP):
        which[k] = 0
    def find(r, n):
        which[n] = jnp.where(live_ref[r] > 0, r, 0)
        return n + live_ref[r]
    lax.fori_loop(0, live_ref.shape[0], find, 0, unroll=True)
    copies = [pltpu.make_async_copy(b_ref.at[which[k]], out_ref.at[k], sems.at[k]) for k in range(B_KEEP)]
    for c in copies: c.start()
    for c in copies: c.wait()

def pack_right(b, live):
    return pl.pallas_call(
        pack_kernel,
        out_shape=jax.ShapeDtypeStruct((B_KEEP, BS, BS), f32),
        in_specs=[pl.BlockSpec(memory_space=pltpu.SMEM), pl.BlockSpec(memory_space=pl.ANY)],
        out_specs=pl.BlockSpec(memory_space=pltpu.VMEM),
        scratch_shapes=[pltpu.SMEM((B_KEEP + 1,), jnp.int32), pltpu.SemaphoreType.DMA((B_KEEP,))],
        name="pack_right",
    )(live, b)

def product_kernel(table_ref, a_live_ref, b_live_ref, a_ref, b_ref, out_ref,
                   total, blocks, weights, rank, left_list, right_list, target_list, sems, out_sem):
    def count(r, n):
        rank[r] = n
        return n + b_live_ref[r]
    lax.fori_loop(0, b_live_ref.shape[0], count, 0, unroll=True)

    def keep(t, n):
        l = table_ref[0, t]; r = table_ref[1, t]; c = table_ref[2, t]
        left_list[n] = l
        right_list[n] = rank[r]
        target_list[n] = c
        useful = a_live_ref[l] * b_live_ref[r]
        return n + jnp.where(c < C_SLOTS, useful, 0)
    n = lax.fori_loop(0, BATCH, keep, 0, unroll=8)
    for u in range(UNROLL):
        left_list[n + u] = 0
        right_list[n + u] = 0
        target_list[n + u] = C_SLOTS
    groups = (n + UNROLL - 1) // UNROLL

    def fetch(g, _):
        for u in range(UNROLL):
            t = g * UNROLL + u
            pltpu.make_async_copy(a_ref.at[left_list[t]], blocks.at[t], sems.at[g]).start()
        return 0
    lax.fori_loop(0, groups, fetch, 0)

    for k in range(B_KEEP):
        b = b_ref[k]
        hi = b.astype(bf16)
        lo = (b - hi.astype(f32)).astype(bf16)
        weights[k, :BS, :BS] = hi
        weights[k, :BS, BS:] = lo
        weights[k, BS:, :BS] = hi
        weights[k, BS:, BS:] = jnp.zeros_like(lo)

    def clear(c, _):
        total[c] = jnp.zeros((BS, BS), f32)
        return 0
    lax.fori_loop(0, C_SLOTS, clear, 0, unroll=4)

    def work(g, _):
        here = pl.ds(g * UNROLL, UNROLL)
        pltpu.make_async_copy(a_ref.at[pl.ds(0, UNROLL)], blocks.at[here], sems.at[g]).wait()
        products = []
        for u in range(UNROLL):
            t = g * UNROLL + u
            a = blocks[t]
            hi = a.astype(bf16)
            lo = (a - hi.astype(f32)).astype(bf16)
            both = jnp.dot(jnp.concatenate([hi, lo], axis=1), weights[right_list[t]], preferred_element_type=f32)
            products.append(both[:, :BS] + both[:, BS:])
        for u in range(UNROLL):
            c = target_list[g * UNROLL + u]
            total[c] = total[c] + products[u]
        return 0
    lax.fori_loop(0, groups, work, 0)
    out = pltpu.make_async_copy(total.at[pl.ds(0, C_SLOTS)], out_ref, out_sem)
    out.start(); out.wait()

def products(a, a_live, b_kept, b_live, table, name):
    most = BATCH + UNROLL
    return pl.pallas_call(
        product_kernel,
        out_shape=jax.ShapeDtypeStruct((C_SLOTS, BS, BS), f32),
        in_specs=[pl.BlockSpec(memory_space=pltpu.SMEM)] * 3
        + [pl.BlockSpec(memory_space=pl.ANY), pl.BlockSpec(memory_space=pltpu.VMEM)],
        out_specs=pl.BlockSpec(memory_space=pl.ANY),
        scratch_shapes=[
            pltpu.VMEM((C_SLOTS + 1, BS, BS), f32),
            pltpu.VMEM((most, BS, BS), f32),
            pltpu.VMEM((B_KEEP, 2 * BS, 2 * BS), bf16),
            pltpu.SMEM((b_live.shape[0],), jnp.int32),
            pltpu.SMEM((most,), jnp.int32), pltpu.SMEM((most,), jnp.int32), pltpu.SMEM((most,), jnp.int32),
            pltpu.SemaphoreType.DMA((most // UNROLL,)),
            pltpu.SemaphoreType.DMA,
        ],
        compiler_params=pltpu.CompilerParams(vmem_limit_bytes=40 * 2**20),
        name=name,
    )(table, a_live, b_live, a, b_kept)


def shards(a_values, b_values, a_live, b_live, triples):
    a, a_on = a_values[0, 0, 0], a_live[0, 0, 0]
    b, b_on = b_values[0, 0, 0], b_live[0, 0, 0]
    tables = triples[0, 0, 0]
    rows, cols = lax.axis_size("row"), lax.axis_size("col")
    to_left = [(i * cols + (j + 1) % cols, (i + 1) % rows * cols + j) for i in range(rows) for j in range(cols)]
    down = [(i, (i + 1) % rows) for i in range(rows)]
    up = [(i, (i - 1) % rows) for i in range(rows)]
    kept = pack_right(b, b_on)
    kept_far = lax.ppermute(kept, ("row", "col"), to_left)
    b_on_far = lax.ppermute(b_on, ("row", "col"), to_left)
    table_far = lax.ppermute(tables[1], "row", down)
    second = products(a, a_on, kept_far, b_on_far, table_far, "second")
    first = products(a, a_on, kept, b_on, tables[0], "first")
    second = lax.ppermute(second, "row", up)
    shares = lax.psum_scatter(first + second, "rep", scatter_dimension=0, tiled=True)
    return shares.reshape(1, 1, C_SLOTS // lax.axis_size("rep"), BS, BS)


def solution(mesh):
    placed = (
        P("row", "col", "rep", None, None, None),
        P("row", "col", "rep", None, None, None),
        P("row", "col", "rep", None),
        P("row", "col", "rep", None),
        P("row", "col", "rep", None, None, None),
    )
    return jax.shard_map(
        shards,
        mesh=mesh,
        in_specs=placed,
        out_specs=P("row", "col", "rep", None, None),
        check_vma=False,
    )
```

```python
import jax
import jax.numpy as jnp
from jax import lax
from jax.experimental import pallas as pl
from jax.experimental.pallas import tpu as pltpu
from jax.sharding import PartitionSpec as P

BS = 128
C_SLOTS = 48
B_KEEP = 8
BATCH = 256
UNROLL = 16
N_ROW = 16
N_REP = 4
SHARE = C_SLOTS // N_REP
HALF = SHARE // 2
f32 = jnp.float32
bf16 = jnp.bfloat16


def pack_kernel(live_ref, b_ref, out_ref, which, sems):
    for k in range(B_KEEP):
        which[k] = 0

    def find(r, n):
        which[n] = jnp.where(live_ref[r] > 0, r, 0)
        return n + live_ref[r]

    lax.fori_loop(0, live_ref.shape[0], find, 0, unroll=True)
    copies = [pltpu.make_async_copy(b_ref.at[which[k]], out_ref.at[k], sems.at[k]) for k in range(B_KEEP)]
    for c in copies:
        c.start()
    for c in copies:
        c.wait()


def pack_right(b, live):
    return pl.pallas_call(
        pack_kernel,
        out_shape=jax.ShapeDtypeStruct((B_KEEP, BS, BS), f32),
        in_specs=[pl.BlockSpec(memory_space=pltpu.SMEM), pl.BlockSpec(memory_space=pl.ANY)],
        out_specs=pl.BlockSpec(memory_space=pltpu.VMEM),
        scratch_shapes=[pltpu.SMEM((B_KEEP + 1,), jnp.int32), pltpu.SemaphoreType.DMA((B_KEEP,))],
        name="pack_right",
    )(live, b)


def product_kernel(extra, parts, far, table_ref, a_live_ref, b_live_ref, a_ref, b_ref, *rest):
    rest = rest[extra:]
    outs = rest[: len(parts)]
    total, weights, rank, moved, left_list, right_list, target_list, out_sems = rest[len(parts):]

    def count(r, n):
        rank[r] = n
        return n + b_live_ref[r]

    lax.fori_loop(0, b_live_ref.shape[0], count, 0, unroll=True)

    layer = lax.axis_index("rep")
    if far:
        row = lax.axis_index("row")
        layer = layer + jnp.where(lax.rem(row, 4) == 2, 1, 0)
    for place, ahead in enumerate((2, 3, 1, 0)):
        owner = lax.rem(layer + ahead, N_REP)
        moved[owner] = (place - owner) * SHARE
    moved[N_REP] = 0

    def keep(t, n):
        l = table_ref[0, t]
        r = table_ref[1, t]
        c = table_ref[2, t]
        left_list[n] = l
        right_list[n] = rank[r]
        target_list[n] = c + moved[(c * 43) >> 9]
        return n + jnp.where(c < C_SLOTS, a_live_ref[l] * b_live_ref[r], 0)

    n = lax.fori_loop(0, BATCH, keep, 0, unroll=8)
    for u in range(UNROLL):
        left_list[n + u] = 0
        right_list[n + u] = 0
        target_list[n + u] = C_SLOTS
    groups = (n + UNROLL - 1) // UNROLL
    for k in range(B_KEEP):
        b = b_ref[k]
        hi = b.astype(bf16)
        lo = (b - hi.astype(f32)).astype(bf16)
        weights[k, :BS, :BS] = hi
        weights[k, :BS, BS:] = lo
        weights[k, BS:, :BS] = hi
        weights[k, BS:, BS:] = jnp.zeros_like(lo)

    def clear(c, _):
        total[c] = jnp.zeros((BS, BS), f32)
        return 0

    lax.fori_loop(0, C_SLOTS, clear, 0, unroll=4)

    def work(g, _):
        for u in range(UNROLL):
            t = g * UNROLL + u
            a = a_ref[left_list[t]]
            hi = a.astype(bf16)
            lo = (a - hi.astype(f32)).astype(bf16)
            both = jnp.dot(
                jnp.concatenate([hi, lo], axis=1), weights[right_list[t]], preferred_element_type=f32
            )
            c = target_list[t]
            total[c] = total[c] + (both[:, :BS] + both[:, BS:])
        return 0

    lax.fori_loop(0, groups, work, 0)
    copies = [
        pltpu.make_async_copy(total.at[pl.ds(at, size)], outs[k], out_sems.at[k]) for k, (at, size) in enumerate(parts)
    ]
    for c in copies:
        c.start()
    for c in copies:
        c.wait()


def products(a, a_live, b_kept, b_live, table, first, parts, far, name):
    most = BATCH + UNROLL

    def kernel(*refs):
        product_kernel(len(first), parts, far, *refs)

    return pl.pallas_call(
        kernel,
        out_shape=[jax.ShapeDtypeStruct((size, BS, BS), f32) for _, size in parts],
        in_specs=[pl.BlockSpec(memory_space=pltpu.SMEM)] * 3
        + [pl.BlockSpec(memory_space=pltpu.VMEM)] * 2
        + [pl.BlockSpec(memory_space=pl.ANY)] * len(first),
        out_specs=[pl.BlockSpec(memory_space=pl.ANY)] * len(parts),
        scratch_shapes=[
            pltpu.VMEM((C_SLOTS + 1, BS, BS), f32),
            pltpu.VMEM((B_KEEP, 2 * BS, 2 * BS), bf16),
            pltpu.SMEM((b_live.shape[0],), jnp.int32),
            pltpu.SMEM((N_REP + 1,), jnp.int32),
            pltpu.SMEM((most,), jnp.int32),
            pltpu.SMEM((most,), jnp.int32),
            pltpu.SMEM((most,), jnp.int32),
            pltpu.SemaphoreType.DMA((len(parts),)),
        ],
        compiler_params=pltpu.CompilerParams(vmem_limit_bytes=26 * 2**20),
        name=name,
    )(table, a_live, b_live, a, b_kept, *first)


def after(x, first, flops=0):
    def kernel(x_ref, first_ref, out_ref):
        pass

    return pl.pallas_call(
        kernel,
        out_shape=jax.ShapeDtypeStruct(x.shape, x.dtype),
        in_specs=[pl.BlockSpec(memory_space=pl.ANY)] * 2,
        out_specs=pl.BlockSpec(memory_space=pl.ANY),
        input_output_aliases={0: 0},
        cost_estimate=pl.CostEstimate(flops=flops, bytes_accessed=0, transcendentals=0),
        name="after",
    )(x, first)


def moves(rule):
    pairs = []
    for x in range(4):
        for z in range(8):
            for core in range(2):
                to = rule(x, z, core)
                if to is not None:
                    ends = [(4 * (u % 4) + 2 * (w % 8 % 2) + c) * N_REP + w % 8 // 2 for u, w, c in ((x, z, core), to)]
                    pairs.append(tuple(ends))
    return pairs


def send(x, rule):
    return lax.ppermute(x, ("row", "rep"), moves(rule))


def to_other_core(x, z, core):
    return (x, z, 0) if core == 1 else None


def to_owner_ring(step):
    def rule(x, z, core):
        if core == 1:
            return None
        return (x if z % 2 == 1 else x - 1, z + step, 1)

    return rule


def layers_on(step, cores):
    def rule(x, z, core):
        return (x, z + 2 * step, core) if core in cores else None

    return rule


def shards(a_values, b_values, a_live, b_live, triples):
    a, a_on = a_values[0, 0, 0], a_live[0, 0, 0]
    b, b_on = b_values[0, 0, 0], b_live[0, 0, 0]
    tables = triples[0, 0, 0]
    rows, cols = lax.axis_size("row"), lax.axis_size("col")
    to_left = [(i * cols + (j + 1) % cols, (i + 1) % rows * cols + j) for i in range(rows) for j in range(cols)]
    next_row = [(i, (i + 1) % rows) for i in range(rows)]
    kept = pack_right(b, b_on)
    kept_far = lax.ppermute(kept, ("row", "col"), to_left)
    b_on_far = lax.ppermute(b_on, ("row", "col"), to_left)
    table_far = lax.ppermute(tables[1], "row", next_row)

    shares_at = [(0, HALF), (HALF, HALF)] + [(k * SHARE, SHARE) for k in range(1, N_REP)]
    own0a, own0b, own_down, own_up, own_here = products(a, a_on, kept, b_on, tables[0], (), shares_at, False, "first")
    shares_at = [(k * SHARE, SHARE) for k in range(N_REP)] + [(SHARE, C_SLOTS - SHARE)]
    far0, far1, far2, far3, rest = products(a, a_on, kept_far, b_on_far, table_far, (own0a,), shares_at, True, "second")
    odd_down = send(far0, to_owner_ring(-1))
    odd_up = send(far2, to_owner_ring(1))
    near0 = send(far0, to_other_core)

    down = own0a + near0[:HALF]
    up = own0b + near0[HALF:]
    near = send(after(rest, down), to_other_core)
    odd_down = after(odd_down, down, 5 * 10**9)
    odd_up = after(odd_up, up, 5 * 10**9)
    down = send(down, layers_on(-1, (0, 1)))
    up = send(up, layers_on(1, (0, 1)))
    late_down = send(after(far1, odd_down), to_owner_ring(-1))
    late_up = send(after(far3, odd_up), to_owner_ring(1))
    nothing = jnp.zeros((HALF, BS, BS), f32)
    down = send(own_down + odd_down + near[:SHARE] + jnp.concatenate([down, nothing]), layers_on(-1, (0, 1)))
    up = send(own_up + odd_up + near[SHARE : 2 * SHARE] + jnp.concatenate([nothing, up]), layers_on(1, (0, 1)))
    shares = own_here + near[2 * SHARE :] + late_down + late_up + down + up
    return shares.reshape(1, 1, SHARE, BS, BS)


def solution(mesh):
    placed = (
        P("row", "col", "rep", None, None, None),
        P("row", "col", "rep", None, None, None),
        P("row", "col", "rep", None),
        P("row", "col", "rep", None),
        P("row", "col", "rep", None, None, None),
    )
    return jax.shard_map(
        shards,
        mesh=mesh,
        in_specs=placed,
        out_specs=P("row", "col", "rep", None, None),
        check_vma=False,
    )
```

```python
import jax
import jax.numpy as jnp
from jax import lax
from jax.experimental import pallas as pl
from jax.experimental.pallas import tpu as pltpu
from jax.sharding import PartitionSpec as P

BS = 128
C_SLOTS = 48
B_KEEP = 8
BATCH = 256
UNROLL = 16
N_ROW = 16
N_REP = 4
SHARE = C_SLOTS // N_REP
HALF = SHARE // 2
f32 = jnp.float32
bf16 = jnp.bfloat16


def pack_kernel(live_ref, b_ref, out_ref, which, sems):
    for k in range(B_KEEP):
        which[k] = 0

    def find(r, n):
        which[n] = jnp.where(live_ref[r] > 0, r, 0)
        return n + live_ref[r]

    lax.fori_loop(0, live_ref.shape[0], find, 0, unroll=True)
    copies = [pltpu.make_async_copy(b_ref.at[which[k]], out_ref.at[k], sems.at[k]) for k in range(B_KEEP)]
    for c in copies:
        c.start()
    for c in copies:
        c.wait()


def pack_right(b, live):
    return pl.pallas_call(
        pack_kernel,
        out_shape=jax.ShapeDtypeStruct((B_KEEP, BS, BS), f32),
        in_specs=[pl.BlockSpec(memory_space=pltpu.SMEM), pl.BlockSpec(memory_space=pl.ANY)],
        out_specs=pl.BlockSpec(memory_space=pltpu.VMEM),
        scratch_shapes=[pltpu.SMEM((B_KEEP + 1,), jnp.int32), pltpu.SemaphoreType.DMA((B_KEEP,))],
        name="pack_right",
    )(live, b)


def product_kernel(extra, parts, far, table_ref, a_live_ref, b_live_ref, a_ref, b_ref, *rest):
    rest = rest[extra:]
    outs = rest[: len(parts)]
    total, weights, rank, moved, left_list, right_list, target_list, out_sems = rest[len(parts):]

    def count(r, n):
        rank[r] = n
        return n + b_live_ref[r]

    lax.fori_loop(0, b_live_ref.shape[0], count, 0, unroll=True)

    layer = lax.axis_index("rep")
    if far:
        row = lax.axis_index("row")
        layer = layer + jnp.where(lax.rem(row, 4) == 2, 1, 0)
    for place, ahead in enumerate((2, 3, 1, 0)):
        owner = lax.rem(layer + ahead, N_REP)
        moved[owner] = (place - owner) * SHARE
    moved[N_REP] = 0

    def keep(t, n):
        l = table_ref[0, t]
        r = table_ref[1, t]
        c = table_ref[2, t]
        left_list[n] = l
        right_list[n] = rank[r]
        target_list[n] = c + moved[(c * 43) >> 9]
        return n + jnp.where(c < C_SLOTS, a_live_ref[l] * b_live_ref[r], 0)

    n = lax.fori_loop(0, BATCH, keep, 0, unroll=8)
    for u in range(UNROLL):
        left_list[n + u] = 0
        right_list[n + u] = 0
        target_list[n + u] = C_SLOTS
    groups = (n + UNROLL - 1) // UNROLL
    for k in range(B_KEEP):
        b = b_ref[k]
        hi = b.astype(bf16)
        lo = (b - hi.astype(f32)).astype(bf16)
        weights[k, :BS, :BS] = hi
        weights[k, :BS, BS:] = lo
        weights[k, BS:, :BS] = hi
        weights[k, BS:, BS:] = jnp.zeros_like(lo)

    def clear(c, _):
        total[c] = jnp.zeros((BS, BS), f32)
        return 0

    lax.fori_loop(0, C_SLOTS, clear, 0, unroll=4)

    def work(g, _):
        for u in range(UNROLL):
            t = g * UNROLL + u
            a = a_ref[left_list[t]]
            hi = a.astype(bf16)
            lo = (a - hi.astype(f32)).astype(bf16)
            both = jnp.dot(
                jnp.concatenate([hi, lo], axis=1), weights[right_list[t]], preferred_element_type=f32
            )
            c = target_list[t]
            total[c] = total[c] + (both[:, :BS] + both[:, BS:])
        return 0

    lax.fori_loop(0, groups, work, 0)
    copies = [
        pltpu.make_async_copy(total.at[pl.ds(at, size)], outs[k], out_sems.at[k]) for k, (at, size) in enumerate(parts)
    ]
    for c in copies:
        c.start()
    for c in copies:
        c.wait()


def products(a, a_live, b_kept, b_live, table, first, parts, far, name):
    most = BATCH + UNROLL

    def kernel(*refs):
        product_kernel(len(first), parts, far, *refs)

    return pl.pallas_call(
        kernel,
        out_shape=[jax.ShapeDtypeStruct((size, BS, BS), f32) for _, size in parts],
        in_specs=[pl.BlockSpec(memory_space=pltpu.SMEM)] * 3
        + [pl.BlockSpec(memory_space=pltpu.VMEM)] * 2
        + [pl.BlockSpec(memory_space=pl.ANY)] * len(first),
        out_specs=[pl.BlockSpec(memory_space=pl.ANY)] * len(parts),
        scratch_shapes=[
            pltpu.VMEM((C_SLOTS + 1, BS, BS), f32),
            pltpu.VMEM((B_KEEP, 2 * BS, 2 * BS), bf16),
            pltpu.SMEM((b_live.shape[0],), jnp.int32),
            pltpu.SMEM((N_REP + 1,), jnp.int32),
            pltpu.SMEM((most,), jnp.int32),
            pltpu.SMEM((most,), jnp.int32),
            pltpu.SMEM((most,), jnp.int32),
            pltpu.SemaphoreType.DMA((len(parts),)),
        ],
        cost_estimate=pl.CostEstimate(flops=10**9 if far else 0, bytes_accessed=0, transcendentals=0),
        compiler_params=pltpu.CompilerParams(vmem_limit_bytes=26 * 2**20),
        name=name,
    )(table, a_live, b_live, a, b_kept, *first)


def after(x, first, flops=0):
    def kernel(x_ref, first_ref, out_ref):
        pass

    return pl.pallas_call(
        kernel,
        out_shape=jax.ShapeDtypeStruct(x.shape, x.dtype),
        in_specs=[pl.BlockSpec(memory_space=pl.ANY)] * 2,
        out_specs=pl.BlockSpec(memory_space=pl.ANY),
        input_output_aliases={0: 0},
        cost_estimate=pl.CostEstimate(flops=flops, bytes_accessed=flops // 300, transcendentals=0),
        name="after",
    )(x, first)


def moves(rule):
    pairs = []
    for x in range(4):
        for z in range(8):
            for core in range(2):
                to = rule(x, z, core)
                if to is not None:
                    ends = [(4 * (u % 4) + 2 * (w % 8 % 2) + c) * N_REP + w % 8 // 2 for u, w, c in ((x, z, core), to)]
                    pairs.append(tuple(ends))
    return pairs


def send(x, rule, name, flops):
    with jax.named_scope(name):
        x = lax.ppermute(x, ("row", "rep"), moves(rule))
        return after(x, lax.axis_index("rep").reshape(1), flops) if flops else x


def to_other_core(x, z, core):
    return (x, z, 0) if core == 1 else None


def to_owner_ring(step):
    def rule(x, z, core):
        if core == 1:
            return None
        return (x if z % 2 == 1 else x - 1, z + step, 1)

    return rule


def layers_on(step, cores):
    def rule(x, z, core):
        return (x, z + 2 * step, core) if core in cores else None

    return rule


def shards(a_values, b_values, a_live, b_live, triples):
    a, a_on = a_values[0, 0, 0], a_live[0, 0, 0]
    b, b_on = b_values[0, 0, 0], b_live[0, 0, 0]
    tables = triples[0, 0, 0]
    rows, cols = lax.axis_size("row"), lax.axis_size("col")
    to_left = [(i * cols + (j + 1) % cols, (i + 1) % rows * cols + j) for i in range(rows) for j in range(cols)]
    next_row = [(i, (i + 1) % rows) for i in range(rows)]
    kept = pack_right(b, b_on)
    with jax.named_scope("right"):
        kept_far = lax.ppermute(kept, ("row", "col"), to_left)
    with jax.named_scope("right_live"):
        b_on_far = lax.ppermute(b_on, ("row", "col"), to_left)
    with jax.named_scope("table"):
        table_far = lax.ppermute(tables[1], "row", next_row)

    shares_at = [(0, HALF), (HALF, HALF)] + [(k * SHARE, SHARE) for k in range(1, N_REP)]
    own0a, own0b, own_down, own_up, own_here = products(a, a_on, kept, b_on, tables[0], (), shares_at, False, "first")
    shares_at = [(k * SHARE, SHARE) for k in range(N_REP)] + [(SHARE, C_SLOTS - SHARE)]
    far0, far1, far2, far3, rest = products(a, a_on, kept_far, b_on_far, table_far, (own0a,), shares_at, True, "second")
    odd_down = send(far0, to_owner_ring(-1), "odd_down", 0)
    odd_up = send(far2, to_owner_ring(1), "odd_up", 0)
    near0 = send(far0, to_other_core, "near0", 0)

    down = own0a + near0[:HALF]
    up = own0b + near0[HALF:]
    near = send(after(rest, down), to_other_core, "near", 10**10)
    half_down = send(down, layers_on(-1, (0, 1)), "half_down", 0)
    half_up = send(up, layers_on(1, (0, 1)), "half_up", 10**13)
    nothing = jnp.zeros((HALF, BS, BS), f32)
    late_down = send(after(far1, odd_down, 0), to_owner_ring(-1), "late_down", 0)
    late_up = send(after(far3, odd_up, 10**10), to_owner_ring(1), "late_up", 0)
    down = own_down + odd_down + near[:SHARE] + jnp.concatenate([half_down, nothing])
    up = own_up + odd_up + near[SHARE : 2 * SHARE] + jnp.concatenate([nothing, half_up])
    down = send(down, layers_on(-1, (0, 1)), "down", 0)
    up = send(up, layers_on(1, (0, 1)), "up", 10**11)
    shares = own_here + near[2 * SHARE :] + late_down + late_up + down + up
    return shares.reshape(1, 1, SHARE, BS, BS)


def solution(mesh):
    placed = (
        P("row", "col", "rep", None, None, None),
        P("row", "col", "rep", None, None, None),
        P("row", "col", "rep", None),
        P("row", "col", "rep", None),
        P("row", "col", "rep", None, None, None),
    )
    return jax.shard_map(
        shards,
        mesh=mesh,
        in_specs=placed,
        out_specs=P("row", "col", "rep", None, None),
        check_vma=False,
    )
```

```python
import jax
import jax.numpy as jnp
from jax import lax
from jax.experimental import pallas as pl
from jax.experimental.pallas import tpu as pltpu
from jax.sharding import PartitionSpec as P

BS = 128
C_SLOTS = 48
B_KEEP = 8
BATCH = 256
UNROLL = 16
RUN = 32
N_ROW = 16
N_REP = 4
SHARE = C_SLOTS // N_REP
HALF = SHARE // 2
f32 = jnp.float32
bf16 = jnp.bfloat16


def pack_kernel(live_ref, b_ref, out_ref, which, sems):
    for k in range(B_KEEP):
        which[k] = 0

    def find(r, n):
        which[n] = jnp.where(live_ref[r] > 0, r, 0)
        return n + live_ref[r]

    lax.fori_loop(0, live_ref.shape[0], find, 0, unroll=True)
    copies = [pltpu.make_async_copy(b_ref.at[which[k]], out_ref.at[k], sems.at[k]) for k in range(B_KEEP)]
    for c in copies:
        c.start()
    for c in copies:
        c.wait()


def pack_right(b, live):
    return pl.pallas_call(
        pack_kernel,
        out_shape=jax.ShapeDtypeStruct((B_KEEP, BS, BS), f32),
        in_specs=[pl.BlockSpec(memory_space=pltpu.SMEM), pl.BlockSpec(memory_space=pl.ANY)],
        out_specs=pl.BlockSpec(memory_space=pltpu.VMEM),
        scratch_shapes=[pltpu.SMEM((B_KEEP + 1,), jnp.int32), pltpu.SemaphoreType.DMA((B_KEEP,))],
        name="pack_right",
    )(live, b)


def product_kernel(extra, parts, far, table_ref, a_live_ref, b_live_ref, a_ref, b_ref, *rest):
    rest = rest[extra:]
    outs = rest[: len(parts)]
    total, weights, rank, moved, left_list, right_list, target_list, out_sems = rest[len(parts):]

    def count(r, n):
        rank[r] = n
        return n + b_live_ref[r]

    lax.fori_loop(0, b_live_ref.shape[0], count, 0, unroll=True)

    layer = lax.axis_index("rep")
    if far:
        row = lax.axis_index("row")
        layer = layer + jnp.where(lax.rem(row, 4) == 2, 1, 0)
    for place, ahead in enumerate((2, 3, 1, 0)):
        owner = lax.rem(layer + ahead, N_REP)
        moved[owner] = (place - owner) * SHARE
    moved[N_REP] = 0

    def keep(t, n):
        l = table_ref[0, t]
        r = table_ref[1, t]
        c = table_ref[2, t]
        left_list[n] = l
        right_list[n] = rank[r]
        target_list[n] = c + moved[(c * 43) >> 9]
        return n + jnp.where(c < C_SLOTS, a_live_ref[l] * b_live_ref[r], 0)

    def keep_run(k, n):
        for u in range(RUN):
            n = keep(k * RUN + u, n)
        return n

    runs = 0
    for k in range(BATCH // RUN):
        runs = runs + jnp.where(table_ref[2, k * RUN] < C_SLOTS, 1, 0)
    n = lax.fori_loop(0, runs, keep_run, 0)
    for u in range(UNROLL):
        left_list[n + u] = 0
        right_list[n + u] = 0
        target_list[n + u] = C_SLOTS
    groups = (n + UNROLL - 1) // UNROLL
    for k in range(B_KEEP):
        b = b_ref[k]
        hi = b.astype(bf16)
        lo = (b - hi.astype(f32)).astype(bf16)
        weights[k, :BS, :BS] = hi
        weights[k, :BS, BS:] = lo
        weights[k, BS:, :BS] = hi
        weights[k, BS:, BS:] = jnp.zeros_like(lo)

    def clear(c, _):
        total[c] = jnp.zeros((BS, BS), f32)
        return 0

    lax.fori_loop(0, C_SLOTS, clear, 0, unroll=4)

    def work(g, _):
        for u in range(UNROLL):
            t = g * UNROLL + u
            a = a_ref[left_list[t]]
            hi = a.astype(bf16)
            lo = (a - hi.astype(f32)).astype(bf16)
            both = jnp.dot(
                jnp.concatenate([hi, lo], axis=1), weights[right_list[t]], preferred_element_type=f32
            )
            c = target_list[t]
            total[c] = total[c] + (both[:, :BS] + both[:, BS:])
        return 0

    lax.fori_loop(0, groups, work, 0)
    copies = [
        pltpu.make_async_copy(total.at[pl.ds(at, size)], outs[k], out_sems.at[k]) for k, (at, size) in enumerate(parts)
    ]
    for c in copies:
        c.start()
    for c in copies:
        c.wait()


def products(a, a_live, b_kept, b_live, table, first, parts, far, name):
    most = BATCH + UNROLL

    def kernel(*refs):
        product_kernel(len(first), parts, far, *refs)

    return pl.pallas_call(
        kernel,
        out_shape=[jax.ShapeDtypeStruct((size, BS, BS), f32) for _, size in parts],
        in_specs=[pl.BlockSpec(memory_space=pltpu.SMEM)] * 3
        + [pl.BlockSpec(memory_space=pltpu.VMEM)] * 2
        + [pl.BlockSpec(memory_space=pl.ANY)] * len(first),
        out_specs=[pl.BlockSpec(memory_space=pl.ANY)] * len(parts),
        scratch_shapes=[
            pltpu.VMEM((C_SLOTS + 1, BS, BS), f32),
            pltpu.VMEM((B_KEEP, 2 * BS, 2 * BS), bf16),
            pltpu.SMEM((b_live.shape[0],), jnp.int32),
            pltpu.SMEM((N_REP + 1,), jnp.int32),
            pltpu.SMEM((most,), jnp.int32),
            pltpu.SMEM((most,), jnp.int32),
            pltpu.SMEM((most,), jnp.int32),
            pltpu.SemaphoreType.DMA((len(parts),)),
        ],
        cost_estimate=pl.CostEstimate(flops=10**9 if far else 0, bytes_accessed=0, transcendentals=0),
        compiler_params=pltpu.CompilerParams(vmem_limit_bytes=26 * 2**20),
        name=name,
    )(table, a_live, b_live, a, b_kept, *first)


def after(x, first, flops=0):
    def kernel(x_ref, first_ref, out_ref):
        pass

    return pl.pallas_call(
        kernel,
        out_shape=jax.ShapeDtypeStruct(x.shape, x.dtype),
        in_specs=[pl.BlockSpec(memory_space=pl.ANY)] * 2,
        out_specs=pl.BlockSpec(memory_space=pl.ANY),
        input_output_aliases={0: 0},
        cost_estimate=pl.CostEstimate(flops=flops, bytes_accessed=flops // 300, transcendentals=0),
        name="after",
    )(x, first)


def moves(rule):
    pairs = []
    for x in range(4):
        for z in range(8):
            for core in range(2):
                to = rule(x, z, core)
                if to is not None:
                    ends = [(4 * (u % 4) + 2 * (w % 8 % 2) + c) * N_REP + w % 8 // 2 for u, w, c in ((x, z, core), to)]
                    pairs.append(tuple(ends))
    return pairs


def send(x, rule, name, flops):
    with jax.named_scope(name):
        x = lax.ppermute(x, ("row", "rep"), moves(rule))
        return after(x, lax.axis_index("rep").reshape(1), flops) if flops else x


def to_other_core(x, z, core):
    return (x, z, 0) if core == 1 else None


def to_owner_ring(step):
    def rule(x, z, core):
        if core == 1:
            return None
        return (x if z % 2 == 1 else x - 1, z + step, 1)

    return rule


def layers_on(step, cores):
    def rule(x, z, core):
        return (x, z + 2 * step, core) if core in cores else None

    return rule


def shards(a_values, b_values, a_live, b_live, triples):
    a, a_on = a_values[0, 0, 0], a_live[0, 0, 0]
    b, b_on = b_values[0, 0, 0], b_live[0, 0, 0]
    tables = triples[0, 0, 0]
    rows, cols = lax.axis_size("row"), lax.axis_size("col")
    to_left = [(i * cols + (j + 1) % cols, (i + 1) % rows * cols + j) for i in range(rows) for j in range(cols)]
    next_row = [(i, (i + 1) % rows) for i in range(rows)]
    kept = pack_right(b, b_on)
    with jax.named_scope("right"):
        kept_far = lax.ppermute(kept, ("row", "col"), to_left)
    with jax.named_scope("right_live"):
        b_on_far = lax.ppermute(b_on, ("row", "col"), to_left)
    with jax.named_scope("table"):
        table_far = lax.ppermute(tables[1], "row", next_row)

    shares_at = [(0, HALF), (HALF, HALF)] + [(k * SHARE, SHARE) for k in range(1, N_REP)]
    own0a, own0b, own_down, own_up, own_here = products(a, a_on, kept, b_on, tables[0], (), shares_at, False, "first")
    shares_at = [(k * SHARE, SHARE) for k in range(N_REP)] + [(SHARE, C_SLOTS - SHARE)]
    far0, far1, far2, far3, rest = products(a, a_on, kept_far, b_on_far, table_far, (own0a,), shares_at, True, "second")
    odd_down = send(far0, to_owner_ring(-1), "odd_down", 0)
    odd_up = send(far2, to_owner_ring(1), "odd_up", 0)
    near0 = send(far0, to_other_core, "near0", 0)

    down = own0a + near0[:HALF]
    up = own0b + near0[HALF:]
    near = send(after(rest, down), to_other_core, "near", 10**10)
    half_down = send(down, layers_on(-1, (0, 1)), "half_down", 0)
    half_up = send(up, layers_on(1, (0, 1)), "half_up", 10**13)
    nothing = jnp.zeros((HALF, BS, BS), f32)
    late_down = send(after(far1, odd_down, 0), to_owner_ring(-1), "late_down", 0)
    late_up = send(after(far3, odd_up, 10**10), to_owner_ring(1), "late_up", 0)
    down = own_down + odd_down + near[:SHARE] + jnp.concatenate([half_down, nothing])
    up = own_up + odd_up + near[SHARE : 2 * SHARE] + jnp.concatenate([nothing, half_up])
    down = send(down, layers_on(-1, (0, 1)), "down", 0)
    up = send(up, layers_on(1, (0, 1)), "up", 10**11)
    shares = own_here + near[2 * SHARE :] + late_down + late_up + down + up
    return shares.reshape(1, 1, SHARE, BS, BS)


def solution(mesh):
    placed = (
        P("row", "col", "rep", None, None, None),
        P("row", "col", "rep", None, None, None),
        P("row", "col", "rep", None),
        P("row", "col", "rep", None),
        P("row", "col", "rep", None, None, None),
    )
    return jax.shard_map(
        shards,
        mesh=mesh,
        in_specs=placed,
        out_specs=P("row", "col", "rep", None, None),
        check_vma=False,
    )
```
